32 devices in a mesh: rows: 8 (over y, x, core), kz: 4 (over z).
Axes of the slice: x: 2, y: 2, z: 4, core: 2. Of those that a mesh axis runs over, the one named last changes fastest.
Arguments:
- velocity: float32 [3, 768, 128, 512], P(None, 'rows', None, 'kz'), may hold values from -6 to 6
- forcing_blocks: bfloat16 [64, 3, 768, 256], P('kz', None, 'rows'), may hold values from -6 to 6
- mode_index: int32 [64], P('kz'), may hold values from 0 to 255
- eigen_rates: float32 [2, 384], replicated, may hold values from 0.1 to 10
- to_modes: float32 [2, 384, 384], replicated, may hold values from -1 to 2
- from_modes: float32 [2, 384, 384], replicated, may hold values from -1 to 2
Outputs:
- velocity_next: float32 [3, 768, 128, 512], P(None, None, 'rows', 'kz')
The draws below stay inside these ranges and needn't reach their ends.
All inputs are finite; a program needn't handle non-finite values.
Results may differ from the reference program's by a relative error of at most 0.0003.
Values may be sent and summed in bfloat16 or wider, within the bound.
A program may use at most 128 MiB of HBM per device.

```python
import math
import jax
import jax.numpy as jnp
from jax import lax

NY = 768
NYH = 384
KX = 128
KZ = 256
FB = 64


def basis_draw(key):
    noise = 0.3 * jax.random.truncated_normal(key, -6.0, 6.0, (2, NYH, NYH), jnp.float32)
    return jnp.eye(NYH, dtype=jnp.float32)[None] + noise / jnp.sqrt(jnp.float32(NYH))


def draw_to_modes(key, part):
    return basis_draw(jax.random.fold_in(key, 11))


def draw_from_modes(key, part):
    return basis_draw(jax.random.fold_in(key, 23))


def set_ends(entries, stream_key, low, largest):
    extent = entries.shape
    spot = [jax.random.randint(jax.random.fold_in(stream_key, axis), (), 0, extent[axis]) for axis in range(len(extent))]
    entries = entries.at[tuple(spot)].set(low)
    longest = extent.index(max(extent))
    spot[longest] = (spot[longest] + 1) % extent[longest]
    return entries.at[tuple(spot)].set(largest)


def steps_of(rng, extent, shards, least, largest):
    factor_of = 1.0
    for dim, blocks in shards:
        steps = jax.random.uniform(jax.random.fold_in(jax.random.fold_in(rng, 6), dim), (blocks,), jnp.float32, least / len(shards), largest / len(shards))
        factor_of = factor_of * jnp.repeat(jnp.exp(steps), extent[dim] // blocks).reshape((-1,) + (1,) * (len(extent) - 1 - dim))
    return factor_of


def centred(rng, dims, spread, bound, cuts=(), held_as=jnp.bfloat16):
    factor_of = steps_of(rng, dims, cuts, -0.22, 0.18) if cuts else 1.0
    drawn = jax.random.normal(rng, dims, jnp.float32) * spread * factor_of
    return jnp.minimum(jnp.maximum(drawn, -bound), bound).astype(held_as)


def setup_inputs(seed: int = 0) -> dict:
    seeds = jax.random.split(jax.random.key(seed), 7)
    velocity = centred(seeds[0], (3, NY, KX, 2 * KZ), 1.0, 6.0, ((1, 8), (3, 4)), jnp.float32)
    forcing_blocks = centred(seeds[1], (FB, 3, NY, 2 * KX), 1.0, 6.0, ((0, 4), (2, 8)))
    mode_index = set_ends(jax.random.randint(seeds[2], (FB,), 0, KZ), jax.random.fold_in(seeds[2], 1), 0, KZ - 1).astype(jnp.int32)
    eigen_rates = jnp.clip(jnp.exp(jax.random.uniform(seeds[3], (2, NYH), jnp.float32, math.log(0.1), math.log(10.0))), 0.1, 10.0)
    to_modes = draw_to_modes(jax.random.fold_in(seeds[6], 71), 0)
    from_modes = draw_from_modes(jax.random.fold_in(seeds[6], 71), 0)
    return {"velocity": velocity, "forcing_blocks": forcing_blocks, "mode_index": mode_index, "eigen_rates": eigen_rates, "to_modes": to_modes, "from_modes": from_modes}


def reference(velocity, forcing_blocks, mode_index, eigen_rates, to_modes, from_modes):
    onehot = (mode_index[:, None] == jnp.arange(KZ, dtype=jnp.int32)[None, :]).astype(jnp.float32)
    kx_scaled = jnp.arange(KX, dtype=jnp.float32) / KX
    kz_scaled = jnp.repeat(jnp.arange(KZ, dtype=jnp.float32) / KZ, 2)
    results = []
    for field_index in range(3):
        blocks = forcing_blocks[:, field_index].astype(jnp.float32).reshape(FB, NY, KX, 2)
        forcing = jnp.einsum("byxc,bm->yxmc", blocks, onehot, precision=lax.Precision.HIGHEST).reshape(NY, KX, 2 * KZ)
        right_side = velocity[field_index] + forcing
        lower_half = right_side[:NYH]
        upper_half = right_side[NYH:]
        parts = ((lower_half + upper_half) * 0.5, (lower_half - upper_half) * 0.5)
        solved = []
        for parity_index in range(2):
            mode_coeff = jnp.einsum("mn,nxz->mxz", to_modes[parity_index], parts[parity_index], precision=lax.Precision.HIGHEST)
            factor = 1.0 / (1.0 + eigen_rates[parity_index][:, None, None] + (kx_scaled ** 2)[None, :, None] + (kz_scaled ** 2)[None, None, :])
            solved.append(jnp.einsum("mn,nxz->mxz", from_modes[parity_index], mode_coeff * factor, precision=lax.Precision.HIGHEST))
        results.append(jnp.concatenate(solved, 0))
    return jnp.stack(results, 0)
```

```python
import functools
import math

import jax
import jax.numpy as jnp
from jax import lax
from jax.experimental import pallas as pl
from jax.experimental.pallas import tpu as pltpu
from jax.sharding import PartitionSpec as P

F32 = jnp.float32
BF16 = jnp.bfloat16
S16 = jnp.int16
FLOOR = 1e-5


def code_steps(bound):
    return 32760.0 / math.log1p(bound / FLOOR)


def encode(value, steps):
    size = steps * jnp.log(1.0 + jnp.abs(value) * (1.0 / FLOOR)) + 0.5
    return jnp.where(value < 0.0, -size, size).astype(jnp.int32).astype(S16)


def decode(code, steps, gain):
    level = code.astype(jnp.int32).astype(F32) * (1.0 / steps)
    size = (jnp.exp(jnp.abs(level)) - 1.0) * (FLOOR * gain)
    return jnp.where(level < 0.0, -size, size)


def spread_kernel(steps, velocity_ref, blocks_ref, onehot_ref, out_ref):
    onehot = onehot_ref[...]
    for y in range(velocity_ref.shape[1]):
        block = blocks_ref[:, y].reshape(onehot.shape[0], blocks_ref.shape[3])
        forcing = lax.dot_general(
            block, onehot, (((0,), (0,)), ((), ())), preferred_element_type=F32
        )
        code = encode(velocity_ref[0, y] + forcing, steps)
        out_ref[:, y] = code.reshape(out_ref.shape[0], out_ref.shape[2], out_ref.shape[3])


def spread(component, velocity, blocks, onehot, row_count, steps, step):
    _, y_count, x_count, z_count = velocity.shape
    x_local = x_count // row_count
    return pl.pallas_call(
        functools.partial(spread_kernel, steps),
        grid=(y_count // step,),
        in_specs=[
            pl.BlockSpec((1, step, x_count, z_count), lambda i: (component, i, 0, 0)),
            pl.BlockSpec(
                (blocks.shape[0], step) + blocks.shape[2:], lambda i: (0, i, 0, 0)
            ),
            pl.BlockSpec(onehot.shape, lambda i: (0, 0)),
        ],
        out_specs=pl.BlockSpec((row_count, step, x_local, z_count), lambda i: (0, i, 0, 0)),
        out_shape=jax.ShapeDtypeStruct((row_count, y_count, x_local, z_count), S16),
        compiler_params=pltpu.CompilerParams(vmem_limit_bytes=40 * 2**20),
        cost_estimate=pl.CostEstimate(
            flops=2 * y_count * x_count * z_count * onehot.shape[0],
            bytes_accessed=y_count * x_count * z_count * 6 + blocks.size * 2,
            transcendentals=0,
        ),
    )(velocity, blocks, onehot)


def split(value):
    high = value.astype(BF16)
    low = (value - high.astype(F32)).astype(BF16)
    return high, low


def weights_of(value):
    high, low = split(value)
    return jnp.concatenate([high, high, low], 1)


def product(weights, value):
    high, low = split(value)
    return jnp.dot(weights, jnp.concatenate([high, low, high], 0), preferred_element_type=F32)


def solve_kernel(steps, width, values_ref, rates_ref, shifts_ref, to_ref, from_ref, *rest):
    out_ref, folded = rest[-2:]
    pair_count = to_ref.shape[1]
    x_count, z_count = shifts_ref.shape
    sign = jnp.where(pl.program_id(0) == 0, 1.0, -1.0).astype(F32)
    chunk = 16

    @pl.loop(0, pair_count // chunk)
    def _(i):
        rows = pl.ds(pl.multiple_of(i * chunk, chunk), chunk)
        uppers = pl.ds(pl.multiple_of(pair_count + i * chunk, chunk), chunk)
        lower = decode(values_ref[rows], steps, 0.5)
        upper = decode(values_ref[uppers], steps, 0.5)
        target = pl.ds(pl.multiple_of(i * chunk * x_count, chunk * x_count), chunk * x_count)
        folded[target] = (lower + sign * upper).reshape(chunk * x_count, z_count)

    to_weights = weights_of(to_ref[0])
    from_weights = weights_of(from_ref[0])
    rates = rates_ref[0]
    for start in range(0, x_count, width):
        columns = range(start, start + width)
        value = jnp.concatenate(
            [folded[pl.ds(x, pair_count, stride=x_count), :] for x in columns], 1
        )
        coeff = product(to_weights, value)
        shift = jnp.concatenate([shifts_ref[x : x + 1, :] for x in columns], 1)
        solved = product(from_weights, coeff * (1.0 / (rates + shift)))
        for k, x in enumerate(columns):
            out_ref[pl.ds(x, pair_count, stride=x_count), :] = solved[
                :, k * z_count : (k + 1) * z_count
            ]


def solve(component, field_count, values, rates, shifts, to_modes, from_modes, previous, steps):
    point_count, x_count, z_count = values.shape
    pair_count = point_count // 2
    specs = [
        pl.BlockSpec(values.shape, lambda p: (0, 0, 0)),
        pl.BlockSpec((1, pair_count, 1), lambda p: (p, 0, 0)),
        pl.BlockSpec(shifts.shape, lambda p: (0, 0)),
        pl.BlockSpec((1, pair_count, pair_count), lambda p: (p, 0, 0)),
        pl.BlockSpec((1, pair_count, pair_count), lambda p: (p, 0, 0)),
    ]
    operands = [values, rates, shifts, to_modes, from_modes]
    aliases = {}
    if previous is not None:
        aliases = {len(operands): 0}
        specs.append(pl.BlockSpec(memory_space=pl.ANY))
        operands.append(previous)
    return pl.pallas_call(
        functools.partial(solve_kernel, steps, 4),
        grid=(2,),
        in_specs=specs,
        out_specs=pl.BlockSpec(
            (pair_count * x_count, z_count), lambda p: (component * 2 + p, 0)
        ),
        out_shape=jax.ShapeDtypeStruct((field_count * point_count * x_count, z_count), F32),
        scratch_shapes=[pltpu.VMEM((pair_count * x_count, z_count), F32)],
        input_output_aliases=aliases,
        compiler_params=pltpu.CompilerParams(vmem_limit_bytes=48 * 2**20),
        cost_estimate=pl.CostEstimate(
            flops=12 * point_count * pair_count * x_count * z_count,
            bytes_accessed=values.size * 6,
            transcendentals=0,
        ),
    )(*operands)


def shards(velocity, forcing_blocks, mode_index, eigen_rates, to_modes, from_modes):
    field_count, y_count, kx_total, column_count = velocity.shape
    mode_count = column_count // 2
    row_count = lax.axis_size("rows")
    kz_count = lax.axis_size("kz")
    kx_local = kx_total // row_count
    block_count = forcing_blocks.shape[0]
    bound = 6.0 * (block_count * kz_count + 1)
    steps = code_steps(bound)

    kz_base = lax.axis_index("kz") * mode_count
    lanes = jnp.arange(2 * kx_total, dtype=jnp.int32)
    swap = (
        lanes[:, None] == (lanes % kx_total * 2 + lanes // kx_total)[None, :]
    ).astype(BF16)
    parts = jnp.einsum("bcyk,kl->cybl", forcing_blocks, swap, preferred_element_type=BF16)
    parts = parts.reshape(field_count, y_count, 2 * block_count, kx_total)
    targets = lax.all_gather(mode_index, "kz", axis=0, tiled=True)
    columns = jnp.arange(column_count, dtype=jnp.int32)
    keys = (2 * targets[:, None] + jnp.arange(2, dtype=jnp.int32)[None, :]).reshape(-1)
    onehot = (keys[:, None] == (2 * kz_base + columns)[None, :]).astype(BF16)

    kz_total = mode_count * kz_count
    kz_scaled = (kz_base + columns // 2).astype(F32) / kz_total
    kx_start = lax.axis_index("rows") * kx_local
    kx_scaled = (kx_start + jnp.arange(kx_local, dtype=jnp.int32)).astype(F32) / kx_total
    shifts = 1.0 + (kx_scaled**2)[:, None] + (kz_scaled**2)[None, :]
    rates = eigen_rates[:, :, None]

    result = None
    for component in range(field_count):
        blocks = lax.all_gather(parts[component], "kz", axis=0, tiled=False)
        sent = spread(component, velocity, blocks, onehot, row_count, steps, 16)
        values = lax.all_to_all(sent, "rows", split_axis=0, concat_axis=0, tiled=True)
        values = values.reshape(row_count * y_count, kx_local, column_count)
        result = solve(
            component, field_count, values, rates, shifts, to_modes, from_modes, result, steps
        )
    return result.reshape(field_count, row_count * y_count, kx_local, column_count)


def solution(mesh):
    return jax.shard_map(
        shards,
        mesh=mesh,
        in_specs=(P(None, "rows", None, "kz"), P("kz", None, "rows", None), P("kz"), P(), P(), P()),
        out_specs=P(None, None, "rows", "kz"),
        check_vma=False,
    )
```

```python
import functools
import math

import jax
import jax.numpy as jnp
from jax import lax
from jax.experimental import pallas as pl
from jax.experimental.pallas import tpu as pltpu
from jax.sharding import PartitionSpec as P

F32 = jnp.float32
BF16 = jnp.bfloat16
S16 = jnp.int16
FLOOR = 1e-5


def code_steps(bound):
    return 32760.0 / math.log1p(bound / FLOOR)


def encode(value, steps):
    size = steps * jnp.log(1.0 + jnp.abs(value) * (1.0 / FLOOR)) + 0.5
    return jnp.where(value < 0.0, -size, size).astype(jnp.int32).astype(S16)


def decode(code, steps, gain):
    level = code.astype(jnp.int32).astype(F32) * (1.0 / steps)
    size = (jnp.exp(jnp.abs(level)) - 1.0) * (FLOOR * gain)
    return jnp.where(level < 0.0, -size, size)


def spread_kernel(steps, count, velocity_ref, onehot_ref, *rest):
    blocks_refs, out_ref = rest[:count], rest[-1]
    onehot = onehot_ref[...]
    for y in range(velocity_ref.shape[1]):
        block = jnp.concatenate(
            [ref[:, y].reshape(-1, ref.shape[3]) for ref in blocks_refs], 0
        )
        forcing = lax.dot_general(
            block, onehot, (((0,), (0,)), ((), ())), preferred_element_type=F32
        )
        code = encode(velocity_ref[0, y] + forcing, steps)
        out_ref[:, y] = code.reshape(out_ref.shape[0], out_ref.shape[2], out_ref.shape[3])


def spread(component, velocity, blocks, onehot, after, row_count, steps, step):
    _, y_count, x_count, z_count = velocity.shape
    x_local = x_count // row_count
    return pl.pallas_call(
        functools.partial(spread_kernel, steps, len(blocks)),
        grid=(y_count // step,),
        in_specs=[
            pl.BlockSpec((1, step, x_count, z_count), lambda i: (component, i, 0, 0)),
            pl.BlockSpec(onehot.shape, lambda i: (0, 0)),
        ]
        + [
            pl.BlockSpec((block.shape[0], step) + block.shape[2:], lambda i: (0, i, 0, 0))
            for block in blocks
        ]
        + [pl.BlockSpec(token.shape, lambda i: (0, 0)) for token in after],
        out_specs=pl.BlockSpec((row_count, step, x_local, z_count), lambda i: (0, i, 0, 0)),
        out_shape=jax.ShapeDtypeStruct((row_count, y_count, x_local, z_count), S16),
        compiler_params=pltpu.CompilerParams(vmem_limit_bytes=40 * 2**20),
        cost_estimate=pl.CostEstimate(
            flops=2 * y_count * x_count * z_count * onehot.shape[0],
            bytes_accessed=y_count * x_count * z_count * 12,
            transcendentals=0,
        ),
    )(velocity, onehot, *blocks, *after)


def split(value):
    high = value.astype(BF16)
    low = (value - high.astype(F32)).astype(BF16)
    return high, low


def weights_of(value):
    high, low = split(value)
    return jnp.concatenate([high, high, low], 1)


def product(weights, value):
    high, low = split(value)
    return jnp.dot(weights, jnp.concatenate([high, low, high], 0), preferred_element_type=F32)


def solve_kernel(steps, width, values_ref, rates_ref, shifts_ref, to_ref, from_ref, *rest):
    out_ref, token_ref, folded = rest[-3:]
    token_ref[...] = jnp.zeros_like(token_ref)
    pair_count = to_ref.shape[1]
    x_count, z_count = shifts_ref.shape
    sign = jnp.where(pl.program_id(0) == 0, 1.0, -1.0).astype(F32)
    chunk = 16

    @pl.loop(0, pair_count // chunk)
    def _(i):
        rows = pl.ds(pl.multiple_of(i * chunk, chunk), chunk)
        uppers = pl.ds(pl.multiple_of(pair_count + i * chunk, chunk), chunk)
        lower = decode(values_ref[rows], steps, 0.5)
        upper = decode(values_ref[uppers], steps, 0.5)
        target = pl.ds(pl.multiple_of(i * chunk * x_count, chunk * x_count), chunk * x_count)
        folded[target] = (lower + sign * upper).reshape(chunk * x_count, z_count)

    to_weights = weights_of(to_ref[0])
    from_weights = weights_of(from_ref[0])
    rates = rates_ref[0]
    for start in range(0, x_count, width):
        columns = range(start, start + width)
        value = jnp.concatenate(
            [folded[pl.ds(x, pair_count, stride=x_count), :] for x in columns], 1
        )
        coeff = product(to_weights, value)
        shift = jnp.concatenate([shifts_ref[x : x + 1, :] for x in columns], 1)
        solved = product(from_weights, coeff * (1.0 / (rates + shift)))
        for k, x in enumerate(columns):
            out_ref[pl.ds(x, pair_count, stride=x_count), :] = solved[
                :, k * z_count : (k + 1) * z_count
            ]


def solve(component, field_count, values, rates, shifts, to_modes, from_modes, previous, steps):
    point_count, x_count, z_count = values.shape
    pair_count = point_count // 2
    specs = [
        pl.BlockSpec(values.shape, lambda p: (0, 0, 0)),
        pl.BlockSpec((1, pair_count, 1), lambda p: (p, 0, 0)),
        pl.BlockSpec(shifts.shape, lambda p: (0, 0)),
        pl.BlockSpec((1, pair_count, pair_count), lambda p: (p, 0, 0)),
        pl.BlockSpec((1, pair_count, pair_count), lambda p: (p, 0, 0)),
    ]
    operands = [values, rates, shifts, to_modes, from_modes]
    aliases = {}
    if previous is not None:
        aliases = {len(operands): 0}
        specs.append(pl.BlockSpec(memory_space=pl.ANY))
        operands.append(previous)
    return pl.pallas_call(
        functools.partial(solve_kernel, steps, 4),
        grid=(2,),
        in_specs=specs,
        out_specs=[
            pl.BlockSpec((pair_count * x_count, z_count), lambda p: (component * 2 + p, 0)),
            pl.BlockSpec((8, z_count), lambda p: (0, 0)),
        ],
        out_shape=[
            jax.ShapeDtypeStruct((field_count * point_count * x_count, z_count), F32),
            jax.ShapeDtypeStruct((8, z_count), F32),
        ],
        scratch_shapes=[pltpu.VMEM((pair_count * x_count, z_count), F32)],
        input_output_aliases=aliases,
        compiler_params=pltpu.CompilerParams(vmem_limit_bytes=48 * 2**20),
        cost_estimate=pl.CostEstimate(
            flops=36 * point_count * pair_count * x_count * z_count,
            bytes_accessed=values.size * 6,
            transcendentals=0,
        ),
    )(*operands)


def shards(velocity, forcing_blocks, mode_index, eigen_rates, to_modes, from_modes):
    field_count, y_count, kx_total, column_count = velocity.shape
    mode_count = column_count // 2
    row_count = lax.axis_size("rows")
    kz_count = lax.axis_size("kz")
    kx_local = kx_total // row_count
    block_count = forcing_blocks.shape[0]
    bound = 6.0 * (block_count * kz_count + 1)
    steps = code_steps(bound)

    kz_base = lax.axis_index("kz") * mode_count
    lanes = jnp.arange(2 * kx_total, dtype=jnp.int32)
    swap = (
        lanes[:, None] == (lanes % kx_total * 2 + lanes // kx_total)[None, :]
    ).astype(BF16)
    targets = lax.all_gather(mode_index, "kz", axis=0, tiled=False)
    columns = jnp.arange(column_count, dtype=jnp.int32)
    reim = jnp.arange(2, dtype=jnp.int32)

    slots = min(8, block_count)
    owners = targets // mode_count
    alike = owners[:, :, None] == owners[:, None, :]
    order = jnp.arange(block_count, dtype=jnp.int32)
    ranks = jnp.sum((alike & (order[None, :] < order[:, None])[None]).astype(jnp.int32), 2)
    fits = jnp.max(ranks) < slots

    kz_total = mode_count * kz_count
    kz_scaled = (kz_base + columns // 2).astype(F32) / kz_total
    kx_start = lax.axis_index("rows") * kx_local
    kx_scaled = (kx_start + jnp.arange(kx_local, dtype=jnp.int32)).astype(F32) / kx_total
    shifts = 1.0 + (kx_scaled**2)[:, None] + (kz_scaled**2)[None, :]
    rates = eigen_rates[:, :, None]

    def pipeline(send, keys):
        onehot = (keys.reshape(-1)[:, None] == (2 * kz_base + columns)[None, :]).astype(BF16)
        result = None
        tokens = []
        for component in range(field_count):
            blocks = send(component)
            sent = spread(
                component, velocity, blocks, onehot, tokens[:-1][-1:], row_count, steps, 16
            )
            values = lax.all_to_all(sent, "rows", split_axis=0, concat_axis=0, tiled=True)
            values = values.reshape(row_count * y_count, kx_local, column_count)
            result, token = solve(
                component, field_count, values, rates, shifts, to_modes, from_modes, result, steps
            )
            tokens.append(token)
        return result

    def some(_):
        mine = lax.axis_index("kz")
        places = jnp.arange(kz_count * slots, dtype=jnp.int32)
        distances = (owners - mine + kz_count) % kz_count
        wanted = lax.dynamic_index_in_dim(distances * slots + ranks, mine, 0, False)
        select = (places[:, None] == wanted[None, :]).astype(BF16)
        picked = jnp.einsum("pb,bcyk->pcyk", select, forcing_blocks, preferred_element_type=BF16)
        parts = jnp.einsum("pcyk,kl->cypl", picked, swap, preferred_element_type=BF16)
        parts = parts.reshape(field_count, y_count, kz_count, 2 * slots, kx_total)
        parts = parts.transpose(0, 2, 1, 3, 4)
        here = (owners == mine)[:, None, :] & (
            ranks[:, None, :] == jnp.arange(slots, dtype=jnp.int32)[None, :, None]
        )
        modes = jnp.sum(jnp.where(here, targets[:, None, :] + 1, 0), 2) - 1
        sources = (mine - jnp.arange(kz_count, dtype=jnp.int32) + kz_count) % kz_count
        modes = modes[sources]
        keys = jnp.where(modes[:, :, None] < 0, -1, 2 * modes[:, :, None] + reim)

        def send(component):
            return [parts[component, :1]] + [
                lax.ppermute(
                    parts[component, distance : distance + 1],
                    "kz",
                    [(source, (source + distance) % kz_count) for source in range(kz_count)],
                )
                for distance in range(1, kz_count)
            ]

        return pipeline(send, keys)

    def every(_):
        parts = jnp.einsum("bcyk,kl->cybl", forcing_blocks, swap, preferred_element_type=BF16)
        parts = parts.reshape(field_count, y_count, 2 * block_count, kx_total)
        keys = 2 * targets[:, :, None] + reim

        def send(component):
            return [lax.all_gather(parts[component], "kz", axis=0, tiled=False)]

        return pipeline(send, keys)

    result = lax.cond(fits, some, every, 0)
    return result.reshape(field_count, row_count * y_count, kx_local, column_count)


def solution(mesh):
    return jax.shard_map(
        shards,
        mesh=mesh,
        in_specs=(P(None, "rows", None, "kz"), P("kz", None, "rows", None), P("kz"), P(), P(), P()),
        out_specs=P(None, None, "rows", "kz"),
        check_vma=False,
    )
```
